768 devices in a mesh: dom: 96 (over y, x, z_hi), ens: 8 (over z_lo, core).
Axes of the slice: x: 4, y: 8, z: 12 (z_hi: 3, z_lo: 4; z = z_hi * 4 + z_lo), core: 2. Of those that a mesh axis runs over, the one named last changes fastest.
Arguments:
- members: bfloat16 [16, 2, 120, 196608], P('ens', None, None, 'dom'), may hold values from -6 to 6
- increment: bfloat16 [2, 120, 196608], P(None, None, 'dom'), may hold values from -6 to 6
- vert_loc: float32 [120, 120], replicated, may hold values from -0.5 to 0.5
- tiles: bfloat16 [48, 4, 128, 128], replicated, may hold values from -0.25 to 0.25
- tile_cols: int32 [48, 4], replicated, may hold values from 0 to 47, as said below
- coarse_of: int32 [196608], P('dom'), may hold values from 0 to 63
Outputs:
- covaried: bfloat16 [2, 120, 196608], P(None, None, ('dom', 'ens'))
The draws below stay inside these ranges and needn't reach their ends.
Inputs may be any that keep to these rules, and one draw needn't show every extreme that they name: `tile_cols`: each row lists 4 different blocks; the first is the row's own block.
All inputs are finite; a program needn't handle non-finite values.
Results may differ from the reference program's by a relative error of at most 0.0049.
Values may be sent and summed in bfloat16 or wider, within the bound.
A program may use at most 32 MiB of HBM per device.

```python
import jax
import jax.numpy as jnp
from jax import lax

VARS = 2
LEV = 120
COL_DEV = 2048
NCO_DEV = 64
TILE = 128
NNZ = 4
MEM = 16
COLS = 196608
NCO = 6144
NB = 48


def draw_tile_cols(key, part):
    key = jax.random.fold_in(key, 5)
    keys = jax.random.split(key, NB)
    offsets = jax.vmap(lambda sub: jax.random.permutation(sub, NB - 1)[:NNZ - 1])(keys) + 1
    first = jnp.zeros((NB, 1), jnp.int32)
    rows = jnp.arange(NB, dtype=jnp.int32)[:, None]
    return ((jnp.concatenate([first, offsets.astype(jnp.int32)], axis=1) + rows) % NB).astype(jnp.int32)


def touch_ends(entries, own_key, least, largest):
    index_at = [jax.random.randint(jax.random.fold_in(own_key, axis), (), 0, length) for axis, length in enumerate(entries.shape)]
    longest = entries.shape.index(max(entries.shape))
    beside = index_at[:longest] + [(index_at[longest] + 1) % entries.shape[longest]] + index_at[longest + 1:]
    return entries.at[tuple(index_at)].set(least).at[tuple(beside)].set(largest)


def shard_levels(rng, shape, cuts, least, largest):
    factor_of, own = 1.0, jax.random.fold_in(rng, 6)
    for dim, parts in cuts:
        draws = jnp.exp(jax.random.uniform(jax.random.fold_in(own, dim), (parts,), jnp.float32, least / len(cuts), largest / len(cuts)))
        factor_of = factor_of * jnp.repeat(draws, shape[dim] // parts).reshape([-1 if axis == dim else 1 for axis in range(len(shape))])
    return factor_of


def bell_draw(rng, extent, width, bound, shards=(), kind=jnp.bfloat16):
    factor_of = shard_levels(rng, extent, shards, -0.22, 0.18) if shards else 1.0
    result = jax.random.normal(rng, extent, jnp.float32) * width * factor_of
    return jnp.minimum(jnp.maximum(result, -bound), bound).astype(kind)


def setup_inputs(seed: int = 0) -> dict:
    key_list = jax.random.split(jax.random.key(seed), 7)
    return {
        "members": bell_draw(key_list[0], (MEM, VARS, LEV, COLS), 1.0, 6.0, ((0, 8), (3, 96))),
        "increment": bell_draw(key_list[1], (VARS, LEV, COLS), 1.0, 6.0, ((2, 96),)),
        "vert_loc": bell_draw(key_list[2], (LEV, LEV), LEV ** -0.5, 0.5, (), jnp.float32),
        "tiles": bell_draw(key_list[3], (NB, NNZ, TILE, TILE), (NNZ * TILE) ** -0.5, 0.25),
        "tile_cols": draw_tile_cols(jax.random.fold_in(key_list[6], 71), 0),
        "coarse_of": touch_ends(jax.random.randint(key_list[5], (COLS,), 0, NCO_DEV), jax.random.fold_in(key_list[5], 1), 0, NCO_DEV - 1).astype(jnp.int32),
    }


def reference(members, increment, vert_loc, tiles, tile_cols, coarse_of):
    highest = lax.Precision.HIGHEST
    glob = (jnp.arange(COLS, dtype=jnp.int32) // COL_DEV) * NCO_DEV + coarse_of
    incr = increment.astype(jnp.float32)

    def one_member(total, member):
        field = member.astype(jnp.float32)
        weighted = field * incr
        vertical = jnp.einsum('lm,cmn->cln', vert_loc, weighted, precision=highest)
        flat = vertical.reshape(VARS * LEV, COLS)
        summed = jax.ops.segment_sum(flat.T, glob, num_segments=NCO).T
        coarse = summed.astype(jnp.bfloat16).astype(jnp.float32)
        blocks = coarse.reshape(VARS * LEV, NB, TILE)
        picked = blocks[:, tile_cols, :]
        smoothed = jnp.einsum('btij,rbtj->rbi', tiles.astype(jnp.float32), picked, precision=highest)
        smoothed = smoothed.reshape(VARS, LEV, NCO)
        back = smoothed[:, :, glob]
        return total + field * back, None

    start = jnp.zeros((VARS, LEV, COLS), jnp.float32)
    total, _ = lax.scan(one_member, start, members)
    return (total / (MEM - 1)).astype(jnp.bfloat16)
```

```python
import jax
import jax.numpy as jnp
from jax import lax
from jax.experimental import pallas as pl
from jax.experimental.pallas import tpu as pltpu
from jax.sharding import PartitionSpec as P

MESH = pl.DeviceIdType.MESH
NY, NX, NZ = 8, 4, 3
NZL = 4
LEV, COLS, NCO = 120, 2048, 64
LG = 16
TILE, NNZ = 128, 4
CH = 512
OC = 256
bf16, f32 = jnp.bfloat16, jnp.float32


def nt(a, b):
    return lax.dot_general(a, b, (((1,), (1,)), ((), ())), preferred_element_type=f32)


def halves(a, b):
    lo = jnp.concatenate([a[:, :NCO], b[:, :NCO]], axis=1)
    hi = jnp.concatenate([a[:, NCO:], b[:, NCO:]], axis=1)
    return lo, hi


def kernel(
    mem_hbm, inc_hbm, vert_ref, tiles_hbm, cols_ref, co_ref, out_ref,
    mem, inc, tl, onehot, s1, r1, s2, r2, blk, s3, r3, pr3, pm, sc, rb,
    in_sem, tl_sem, y_send, y_recv, w_send, w_recv, b_send, b_recv,
    pm_send, pm_recv, p_send, p_recv, c_send, c_recv,
):
    d = lax.axis_index("dom")
    e = lax.axis_index("ens")
    y, x, z = d // (NX * NZ), (d // NZ) % NX, d % NZ
    zl, core = e // 2, e % 2

    def dom(yy, xx, zz):
        return (yy * NX + xx) * NZ + zz

    partner = (d, zl * 2 + 1 - core)
    y_peers = [(y + i) % NY for i in (4, 3, 5, 2, 6, 1, 7)]
    w_peers = [((x + i) % NX, (z + k) % NZ) for i in (2, 1, 3, 0) for k in (1, 2, 0) if i or k]
    b_peers = [((y + i) % NY, (x + k) % NX) for i in (4, 3, 5, 2, 6, 1, 7, 0) for k in (2, 1, 3, 0)]

    steps = COLS // CH
    loads = []
    for i in range(steps):
        at = pl.ds(i * CH, CH)
        a = pltpu.make_async_copy(mem_hbm.at[:, :, at], mem.at[:, :, at], in_sem.at[i, 0])
        b = pltpu.make_async_copy(inc_hbm.at[:, :, at], inc.at[:, :, at], in_sem.at[i, 1])
        a.start()
        b.start()
        loads.append((a, b))

    barrier = pltpu.get_barrier_semaphore()
    greet = [(dom(yy, x, z), e) for yy in y_peers]
    greet += [(dom(y, xx, zz), e) for xx, zz in w_peers]
    greet += [(dom((y + i) % NY, (x + k) % NX, z), e) for i in range(1, NY) for k in range(1, NX)]
    greet += [(d, ((zl + i) % NZL) * 2 + core) for i in range(1, NZL)]
    greet += [partner]
    for peer in greet:
        pl.semaphore_signal(barrier, inc=1, device_id=peer, device_id_type=MESH)

    def tile_load(n):
        dd = dom(n // NX, n % NX, z)
        return pltpu.make_async_copy(
            tiles_hbm.at[dd // 2, :, pl.ds(pl.multiple_of((dd % 2) * NCO, NCO), NCO), :],
            tl.at[n],
            tl_sem,
        )

    def start_tile(n, _):
        tile_load(n).start()
        return 0

    lax.fori_loop(0, NY * NX, start_tile, 0)

    points = lax.broadcasted_iota(jnp.int32, (NCO, COLS), 0)
    onehot[...] = (points == co_ref[...]).astype(f32).astype(bf16)
    sums = [jnp.zeros((LEV, NCO), f32) for _ in range(4)]
    for i in range(steps):
        at = pl.ds(i * CH, CH)
        for a in loads[i]:
            a.wait()
        hot = onehot[:, at]
        for s in range(4):
            w = mem[s, :, at].astype(f32) * inc[s % 2, :, at].astype(f32)
            hi = w.astype(bf16)
            lo = (w - hi.astype(f32)).astype(bf16)
            sums[s] = sums[s] + (nt(hi, hot) + nt(lo, hot))
    summed = jnp.concatenate(sums, axis=1)
    coarse = lax.dot_general(
        vert_ref[...], summed, (((1,), (0,)), ((), ())),
        precision=lax.Precision.HIGHEST, preferred_element_type=f32,
    )
    coarse = jnp.concatenate([coarse, jnp.zeros((NY * LG - LEV, 4 * NCO), f32)], axis=0).astype(bf16)
    for g in range(NY):
        for p in range(2):
            s1[g, p] = coarse[g * LG:(g + 1) * LG, p * 128:(p + 1) * 128]

    pl.semaphore_wait(barrier, len(greet))

    for yy in y_peers:
        pltpu.make_async_remote_copy(
            src_ref=s1.at[yy], dst_ref=r1.at[y], send_sem=y_send, recv_sem=y_recv,
            device_id=(dom(yy, x, z), e), device_id_type=MESH,
        ).start()
    r1[y] = s1[y]
    for q in range(NZL):
        pltpu.make_async_remote_copy(
            src_ref=mem.at[:, :, pl.ds(pl.multiple_of((q * 2 + 1 - core) * OC, OC), OC)],
            dst_ref=pm.at[q], send_sem=pm_send.at[q], recv_sem=pm_recv.at[q],
            device_id=partner, device_id_type=MESH,
        ).start()
    s3[...] = jnp.zeros_like(s3)
    arrived = r1.at[pl.ds(0, NY - 1)]
    pltpu.make_async_copy(arrived, arrived, y_recv).wait()

    for p in range(2):
        for j in range(NY // 2):
            lo, hi = halves(r1[2 * j, p], r1[2 * j + 1, p])
            s2[2 * p, j] = lo
            s2[2 * p + 1, j] = hi
    own = x * NZ + z
    for xx, zz in w_peers:
        pltpu.make_async_remote_copy(
            src_ref=s2.at[xx], dst_ref=r2.at[own], send_sem=w_send, recv_sem=w_recv,
            device_id=(dom(y, xx, zz), e), device_id_type=MESH,
        ).start()
    r2[own] = s2[x]
    arrived = r2.at[pl.ds(0, NX * NZ - 1)]
    pltpu.make_async_copy(arrived, arrived, w_recv).wait()

    for j in range(NY // 2):
        for v in range(NX * NZ // 2):
            lo, hi = halves(r2[2 * v, j], r2[2 * v + 1, j])
            blk[2 * j * (NX * NZ // 2) + v] = lo
            blk[(2 * j + 1) * (NX * NZ // 2) + v] = hi
    pltpu.make_async_copy(tl, tl, tl_sem).wait()
    slot = x * NY + y
    for yy, xx in b_peers:
        n = yy * NX + xx
        b = dom(yy, xx, z) // 2
        picked = jnp.concatenate([blk[cols_ref[b, t]] for t in range(NNZ)], axis=1)
        matrix = jnp.concatenate([tl[n, t] for t in range(NNZ)], axis=1)
        s3[n, :, :NCO] = nt(picked, matrix).astype(bf16)
        if (yy, xx) is not b_peers[-1]:
            pass
    for yy, xx in b_peers[:-1]:
        pltpu.make_async_remote_copy(
            src_ref=s3.at[yy * NX + xx], dst_ref=r3.at[slot], send_sem=b_send, recv_sem=b_recv,
            device_id=(dom(yy, xx, z), e), device_id_type=MESH,
        ).start()
    r3[slot] = s3[y * NX + x]
    arrived = r3.at[pl.ds(0, NY * NX - 1)]
    pltpu.make_async_copy(arrived, arrived, b_recv).wait()

    swap = pltpu.make_async_remote_copy(
        src_ref=r3, dst_ref=pr3, send_sem=p_send, recv_sem=p_recv,
        device_id=partner, device_id_type=MESH,
    )
    swap.start()

    def term(s, fields, local, hot):
        lhs = local[s * NY:(s + 1) * NY].reshape(NY * LG, 128)[:, :NCO]
        back = jnp.dot(lhs, hot, preferred_element_type=f32)
        return fields.astype(f32) * back[:LEV]

    far = zl // 2
    targets = [3 * (1 - far), 2 - far, zl + 1 - 2 * (zl % 2), zl]
    kept = None
    for i, q in enumerate(targets):
        at = pl.ds(pl.multiple_of((q * 2 + core) * OC, OC), OC)
        hot = onehot[:, at]
        parts = [sum(term(k * 2 + c, mem[k * 2 + c, :, at], r3, hot) for k in range(2)) for c in range(2)]
        if i == 0:
            swap.wait_recv()
            for j in range(NZL):
                pltpu.make_async_copy(pm.at[j], pm.at[j], pm_recv.at[j]).wait()
        for c in range(2):
            parts[c] = parts[c] + sum(term(k * 2 + c, pm[q, k * 2 + c], pr3, hot) for k in range(2))
        both = jnp.concatenate(parts, axis=0)
        if i < NZL - 1:
            sc[i] = both.astype(bf16)
            pltpu.make_async_remote_copy(
                src_ref=sc.at[i], dst_ref=rb.at[zl], send_sem=c_send.at[i], recv_sem=c_recv.at[zl],
                device_id=(d, q * 2 + core), device_id_type=MESH,
            ).start()
        else:
            kept = both
    for i in (1, 3, 2):
        j = (zl + i) % NZL
        pltpu.make_async_copy(rb.at[j], rb.at[j], c_recv.at[j]).wait()
        kept = kept + rb[j].astype(f32)
    kept = (kept / 15.0).astype(bf16)
    out_ref[0] = kept[:LEV]
    out_ref[1] = kept[LEV:]

    for ref, count, sem in ((r1, NY - 1, y_send), (r2, NX * NZ - 1, w_send), (r3, NY * NX - 1, b_send)):
        sent = ref.at[pl.ds(0, count)]
        pltpu.make_async_copy(sent, sent, sem).wait()
    for q in range(NZL):
        pltpu.make_async_copy(pm.at[q], pm.at[q], pm_send.at[q]).wait()
    swap.wait_send()
    for i in range(NZL - 1):
        pltpu.make_async_copy(sc.at[i], sc.at[i], c_send.at[i]).wait()


def shards(members, increment, vert_loc, tiles, tile_cols, coarse_of):
    dma = pltpu.SemaphoreType.DMA
    vmem = pl.BlockSpec(memory_space=pltpu.VMEM)
    hbm = pl.BlockSpec(memory_space=pl.ANY)
    return pl.pallas_call(
        kernel,
        name="covary",
        out_shape=jax.ShapeDtypeStruct((2, LEV, OC), bf16),
        in_specs=[hbm, hbm, vmem, hbm, pl.BlockSpec(memory_space=pltpu.SMEM), vmem],
        out_specs=vmem,
        scratch_shapes=[
            pltpu.VMEM((4, LEV, COLS), bf16),
            pltpu.VMEM((2, LEV, COLS), bf16),
            pltpu.VMEM((NY * NX, NNZ, NCO, TILE), bf16),
            pltpu.VMEM((NCO, COLS), bf16),
            pltpu.VMEM((NY, 2, LG, 128), bf16),
            pltpu.VMEM((NY, 2, LG, 128), bf16),
            pltpu.VMEM((NX, NY // 2, LG, 128), bf16),
            pltpu.VMEM((NX * NZ, NY // 2, LG, 128), bf16),
            pltpu.VMEM((NY * NX * NZ // 2, LG, 128), bf16),
            pltpu.VMEM((NY * NX, LG, 128), bf16),
            pltpu.VMEM((NY * NX, LG, 128), bf16),
            pltpu.VMEM((NY * NX, LG, 128), bf16),
            pltpu.VMEM((NZL, 4, LEV, OC), bf16),
            pltpu.VMEM((NZL - 1, 2 * LEV, OC), bf16),
            pltpu.VMEM((NZL, 2 * LEV, OC), bf16),
            dma((COLS // CH, 2)), dma,
            dma, dma, dma, dma, dma, dma,
            dma((NZL,)), dma((NZL,)), dma, dma, dma((NZL - 1,)), dma((NZL,)),
        ],
        compiler_params=pltpu.CompilerParams(
            collective_id=0, has_side_effects=True, vmem_limit_bytes=40 * 2**20
        ),
    )(
        members.reshape(4, LEV, COLS), increment, vert_loc, tiles, tile_cols,
        coarse_of.reshape(1, COLS),
    )


def solution(mesh):
    return jax.shard_map(
        shards,
        mesh=mesh,
        in_specs=(P("ens", None, None, "dom"), P(None, None, "dom"), P(), P(), P(), P("dom")),
        out_specs=P(None, None, ("dom", "ens")),
        check_vma=False,
    )
```

```python
import jax
import jax.numpy as jnp
from jax import lax
from jax.experimental import pallas as pl
from jax.experimental.pallas import tpu as pltpu
from jax.sharding import PartitionSpec as P

MESH = pl.DeviceIdType.MESH
NY, NX, NZ = 8, 4, 3
NZL = 4
LEV, COLS, NCO = 120, 2048, 64
LG = 16
TILE, NNZ = 128, 4
CH = 512
OC = 256
bf16, f32 = jnp.bfloat16, jnp.float32


def nt(a, b):
    return lax.dot_general(a, b, (((1,), (1,)), ((), ())), preferred_element_type=f32)


def halves(a, b):
    lo = jnp.concatenate([a[:, :NCO], b[:, :NCO]], axis=1)
    hi = jnp.concatenate([a[:, NCO:], b[:, NCO:]], axis=1)
    return lo, hi


def kernel(
    mem_hbm, inc_hbm, vert_hbm, tiles_hbm, cols_hbm, co_hbm, out_ref,
    vert_ref, cols_ref, co_ref, mem, inc, tl, onehot, s1, r1, s2, r2, blk, s3, r3, pr3, pm, sc, rb,
    small_sem, in_sem, tl_sem, y_send, y_recv, w_send, w_recv, b_send, b_recv,
    pm_send, pm_recv, p_send, p_recv, c_send, c_recv,
):
    d = lax.axis_index("dom")
    e = lax.axis_index("ens")
    y, x, z = d // (NX * NZ), (d // NZ) % NX, d % NZ
    zl, core = e // 2, e % 2

    def dom(yy, xx, zz):
        return (yy * NX + xx) * NZ + zz

    partner = (d, zl * 2 + 1 - core)
    y_peers = [(y + i) % NY for i in (4, 3, 5, 2, 6, 1, 7)]
    w_peers = [((x + i) % NX, (z + k) % NZ) for i in (2, 1, 3, 0) for k in (1, 2, 0) if i or k]
    b_peers = [((y + i) % NY, (x + k) % NX) for i in (4, 3, 5, 2, 6, 1, 7, 0) for k in (2, 1, 3, 0)]

    small = [
        pltpu.make_async_copy(src, dst, small_sem.at[i])
        for i, (src, dst) in enumerate(((co_hbm, co_ref), (vert_hbm, vert_ref), (cols_hbm, cols_ref)))
    ]
    for copy in small:
        copy.start()
    steps = COLS // CH
    loads = []
    for i in range(steps):
        at = pl.ds(i * CH, CH)
        a = pltpu.make_async_copy(mem_hbm.at[:, :, at], mem.at[:, :, at], in_sem.at[i, 0])
        b = pltpu.make_async_copy(inc_hbm.at[:, :, at], inc.at[:, :, at], in_sem.at[i, 1])
        a.start()
        b.start()
        loads.append((a, b))

    barrier = pltpu.get_barrier_semaphore()
    greet = [(dom(yy, x, z), e) for yy in y_peers]
    greet += [(dom(y, xx, zz), e) for xx, zz in w_peers]
    greet += [(dom((y + i) % NY, (x + k) % NX, z), e) for i in range(1, NY) for k in range(1, NX)]
    greet += [(d, ((zl + i) % NZL) * 2 + core) for i in range(1, NZL)]
    greet += [partner]
    for peer in greet:
        pl.semaphore_signal(barrier, inc=1, device_id=peer, device_id_type=MESH)

    def tile_load(n):
        dd = dom(n // NX, n % NX, z)
        return pltpu.make_async_copy(
            tiles_hbm.at[dd // 2, :, pl.ds(pl.multiple_of((dd % 2) * NCO, NCO), NCO), :],
            tl.at[n],
            tl_sem,
        )

    def start_tile(n, _):
        tile_load(n).start()
        return 0

    lax.fori_loop(0, NY * NX, start_tile, 0)

    small[0].wait()
    points = lax.broadcasted_iota(jnp.int32, (NCO, COLS), 0)
    onehot[...] = (points == co_ref[...]).astype(f32).astype(bf16)
    sums = [jnp.zeros((LEV, NCO), f32) for _ in range(4)]
    for i in range(steps):
        at = pl.ds(i * CH, CH)
        for a in loads[i]:
            a.wait()
        hot = onehot[:, at]
        for s in range(4):
            w = mem[s, :, at].astype(f32) * inc[s % 2, :, at].astype(f32)
            hi = w.astype(bf16)
            lo = (w - hi.astype(f32)).astype(bf16)
            sums[s] = sums[s] + (nt(hi, hot) + nt(lo, hot))
    small[1].wait()
    summed = jnp.concatenate(sums, axis=1)
    coarse = lax.dot_general(
        vert_ref[...], summed, (((1,), (0,)), ((), ())),
        precision=lax.Precision.HIGHEST, preferred_element_type=f32,
    )
    coarse = jnp.concatenate([coarse, jnp.zeros((NY * LG - LEV, 4 * NCO), f32)], axis=0).astype(bf16)
    for g in range(NY):
        for p in range(2):
            s1[g, p] = coarse[g * LG:(g + 1) * LG, p * 128:(p + 1) * 128]

    pl.semaphore_wait(barrier, len(greet))

    for yy in y_peers:
        pltpu.make_async_remote_copy(
            src_ref=s1.at[yy], dst_ref=r1.at[y], send_sem=y_send, recv_sem=y_recv,
            device_id=(dom(yy, x, z), e), device_id_type=MESH,
        ).start()
    r1[y] = s1[y]
    s3[...] = jnp.zeros_like(s3)
    arrived = r1.at[pl.ds(0, NY - 1)]
    pltpu.make_async_copy(arrived, arrived, y_recv).wait()

    for p in range(2):
        for j in range(NY // 2):
            lo, hi = halves(r1[2 * j, p], r1[2 * j + 1, p])
            s2[2 * p, j] = lo
            s2[2 * p + 1, j] = hi
    own = x * NZ + z
    for xx, zz in w_peers:
        pltpu.make_async_remote_copy(
            src_ref=s2.at[xx], dst_ref=r2.at[own], send_sem=w_send, recv_sem=w_recv,
            device_id=(dom(y, xx, zz), e), device_id_type=MESH,
        ).start()
    r2[own] = s2[x]
    for q in range(NZL):
        pltpu.make_async_remote_copy(
            src_ref=mem.at[:, :, pl.ds(pl.multiple_of((q * 2 + 1 - core) * OC, OC), OC)],
            dst_ref=pm.at[q], send_sem=pm_send.at[q], recv_sem=pm_recv.at[q],
            device_id=partner, device_id_type=MESH,
        ).start()
    arrived = r2.at[pl.ds(0, NX * NZ - 1)]
    pltpu.make_async_copy(arrived, arrived, w_recv).wait()

    for j in range(NY // 2):
        for v in range(NX * NZ // 2):
            lo, hi = halves(r2[2 * v, j], r2[2 * v + 1, j])
            blk[2 * j * (NX * NZ // 2) + v] = lo
            blk[(2 * j + 1) * (NX * NZ // 2) + v] = hi
    pltpu.make_async_copy(tl, tl, tl_sem).wait()
    small[2].wait()
    slot = x * NY + y
    for yy, xx in b_peers:
        n = yy * NX + xx
        b = dom(yy, xx, z) // 2
        picked = jnp.concatenate([blk[cols_ref[t, b]] for t in range(NNZ)], axis=1)
        matrix = jnp.concatenate([tl[n, t] for t in range(NNZ)], axis=1)
        s3[n, :, :NCO] = nt(picked, matrix).astype(bf16)
    for yy, xx in b_peers[:-1]:
        pltpu.make_async_remote_copy(
            src_ref=s3.at[yy * NX + xx], dst_ref=r3.at[slot], send_sem=b_send, recv_sem=b_recv,
            device_id=(dom(yy, xx, z), e), device_id_type=MESH,
        ).start()
    r3[slot] = s3[y * NX + x]
    arrived = r3.at[pl.ds(0, NY * NX - 1)]
    pltpu.make_async_copy(arrived, arrived, b_recv).wait()

    swap = pltpu.make_async_remote_copy(
        src_ref=r3, dst_ref=pr3, send_sem=p_send, recv_sem=p_recv,
        device_id=partner, device_id_type=MESH,
    )
    swap.start()

    def term(s, fields, local, hot):
        lhs = local[s * NY:(s + 1) * NY].reshape(NY * LG, 128)[:, :NCO]
        back = jnp.dot(lhs, hot, preferred_element_type=f32)
        return fields.astype(f32) * back[:LEV]

    far = zl // 2
    targets = [3 * (1 - far), 2 - far, zl + 1 - 2 * (zl % 2), zl]
    kept = None
    for i, q in enumerate(targets):
        at = pl.ds(pl.multiple_of((q * 2 + core) * OC, OC), OC)
        hot = onehot[:, at]
        parts = [sum(term(k * 2 + c, mem[k * 2 + c, :, at], r3, hot) for k in range(2)) for c in range(2)]
        if i == 0:
            swap.wait_recv()
            for j in range(NZL):
                pltpu.make_async_copy(pm.at[j], pm.at[j], pm_recv.at[j]).wait()
        for c in range(2):
            parts[c] = parts[c] + sum(term(k * 2 + c, pm[q, k * 2 + c], pr3, hot) for k in range(2))
        both = jnp.concatenate(parts, axis=0)
        if i < NZL - 1:
            sc[i] = both.astype(bf16)
            pltpu.make_async_remote_copy(
                src_ref=sc.at[i], dst_ref=rb.at[zl], send_sem=c_send.at[i], recv_sem=c_recv.at[zl],
                device_id=(d, q * 2 + core), device_id_type=MESH,
            ).start()
        else:
            kept = both
    for i in (1, 3, 2):
        j = (zl + i) % NZL
        pltpu.make_async_copy(rb.at[j], rb.at[j], c_recv.at[j]).wait()
        kept = kept + rb[j].astype(f32)
    kept = (kept / 15.0).astype(bf16)
    out_ref[0] = kept[:LEV]
    out_ref[1] = kept[LEV:]

    for ref, count, sem in ((r1, NY - 1, y_send), (r2, NX * NZ - 1, w_send), (r3, NY * NX - 1, b_send)):
        sent = ref.at[pl.ds(0, count)]
        pltpu.make_async_copy(sent, sent, sem).wait()
    for q in range(NZL):
        pltpu.make_async_copy(pm.at[q], pm.at[q], pm_send.at[q]).wait()
    swap.wait_send()
    for i in range(NZL - 1):
        pltpu.make_async_copy(sc.at[i], sc.at[i], c_send.at[i]).wait()


def shards(members, increment, vert_loc, tiles, tile_cols, coarse_of):
    dma = pltpu.SemaphoreType.DMA
    vmem = pl.BlockSpec(memory_space=pltpu.VMEM)
    hbm = pl.BlockSpec(memory_space=pl.ANY)
    return pl.pallas_call(
        kernel,
        name="covary",
        out_shape=jax.ShapeDtypeStruct((2, LEV, OC), bf16),
        in_specs=[hbm] * 6,
        out_specs=vmem,
        scratch_shapes=[
            pltpu.VMEM((LEV, LEV), f32),
            pltpu.SMEM((NNZ, NY * NX * NZ // 2), jnp.int32),
            pltpu.VMEM((1, COLS), jnp.int32),
            pltpu.VMEM((4, LEV, COLS), bf16),
            pltpu.VMEM((2, LEV, COLS), bf16),
            pltpu.VMEM((NY * NX, NNZ, NCO, TILE), bf16),
            pltpu.VMEM((NCO, COLS), bf16),
            pltpu.VMEM((NY, 2, LG, 128), bf16),
            pltpu.VMEM((NY, 2, LG, 128), bf16),
            pltpu.VMEM((NX, NY // 2, LG, 128), bf16),
            pltpu.VMEM((NX * NZ, NY // 2, LG, 128), bf16),
            pltpu.VMEM((NY * NX * NZ // 2, LG, 128), bf16),
            pltpu.VMEM((NY * NX, LG, 128), bf16),
            pltpu.VMEM((NY * NX, LG, 128), bf16),
            pltpu.VMEM((NY * NX, LG, 128), bf16),
            pltpu.VMEM((NZL, 4, LEV, OC), bf16),
            pltpu.VMEM((NZL - 1, 2 * LEV, OC), bf16),
            pltpu.VMEM((NZL, 2 * LEV, OC), bf16),
            dma((3,)), dma((COLS // CH, 2)), dma,
            dma, dma, dma, dma, dma, dma,
            dma((NZL,)), dma((NZL,)), dma, dma, dma((NZL - 1,)), dma((NZL,)),
        ],
        compiler_params=pltpu.CompilerParams(
            collective_id=0, has_side_effects=True, vmem_limit_bytes=63 * 2**20
        ),
    )(
        members.reshape(4, LEV, COLS), increment, vert_loc, tiles, tile_cols.T,
        coarse_of.reshape(1, COLS),
    )


def solution(mesh):
    return jax.shard_map(
        shards,
        mesh=mesh,
        in_specs=(P("ens", None, None, "dom"), P(None, None, "dom"), P(), P(), P(), P("dom")),
        out_specs=P(None, None, ("dom", "ens")),
        check_vma=False,
    )
```

```python
import jax
import jax.numpy as jnp
from jax import lax
from jax.experimental import pallas as pl
from jax.experimental.pallas import tpu as pltpu
from jax.sharding import PartitionSpec as P

MESH = pl.DeviceIdType.MESH
NY, NX, NZ = 8, 4, 3
NZL = 4
LEV, COLS, NCO = 120, 2048, 64
LG = 16
TILE, NNZ = 128, 4
CH = 512
OC = 256
bf16, f32 = jnp.bfloat16, jnp.float32


def nt(a, b):
    return lax.dot_general(a, b, (((1,), (1,)), ((), ())), preferred_element_type=f32)


def halves(a, b):
    lo = jnp.concatenate([a[:, :NCO], b[:, :NCO]], axis=1)
    hi = jnp.concatenate([a[:, NCO:], b[:, NCO:]], axis=1)
    return lo, hi


def kernel(
    mem_hbm, inc_hbm, vert_hbm, tiles_hbm, cols_hbm, co_hbm, out_ref,
    vert_ref, cols_ref, co_ref, mem, inc, tl, onehot, s1, r1, s2, r2, blk, s3, r3, pr3, pm, sc, rb,
    small_sem, in_sem, tl_sem, y_send, y_recv, w_send, w_recv, b_send, b_recv,
    pm_send, pm_recv, p_send, p_recv, c_send, c_recv, ready,
):
    d = lax.axis_index("dom")
    e = lax.axis_index("ens")
    y, x, z = d // (NX * NZ), (d // NZ) % NX, d % NZ
    zl, core = e // 2, e % 2

    def dom(yy, xx, zz):
        return (yy * NX + xx) * NZ + zz

    partner = (d, zl * 2 + 1 - core)
    y_peers = [(y + i) % NY for i in (4, 3, 5, 2, 6, 1, 7)]
    w_peers = [((x + i) % NX, (z + k) % NZ) for i in (2, 1, 3, 0) for k in (1, 2, 0) if i or k]
    b_peers = [((y + i) % NY, (x + k) % NX) for i in (4, 3, 5, 2, 6, 1, 7, 0) for k in (2, 1, 3, 0)]

    small = [
        pltpu.make_async_copy(src, dst, small_sem.at[i])
        for i, (src, dst) in enumerate(((co_hbm, co_ref), (vert_hbm, vert_ref), (cols_hbm, cols_ref)))
    ]
    for copy in small:
        copy.start()
    steps = COLS // CH
    loads = []
    for i in range(steps):
        at = pl.ds(i * CH, CH)
        a = pltpu.make_async_copy(mem_hbm.at[:, :, at], mem.at[:, :, at], in_sem.at[i, 0])
        b = pltpu.make_async_copy(inc_hbm.at[:, :, at], inc.at[:, :, at], in_sem.at[i, 1])
        a.start()
        b.start()
        loads.append((a, b))

    barrier = pltpu.get_barrier_semaphore()
    greet = [(dom(yy, x, z), e) for yy in y_peers]
    greet += [(dom(y, (x + i) % NX, z), e) for i in range(1, NX)]
    greet += [(dom(y, x, (z + i) % NZ), e) for i in range(1, NZ)]
    greet += [(d, ((zl + i) % NZL) * 2 + core) for i in range(1, NZL)]
    greet += [partner]
    for peer in greet:
        pl.semaphore_signal(barrier, inc=1, device_id=peer, device_id_type=MESH)

    def tile_load(n):
        dd = dom(n // NX, n % NX, z)
        return pltpu.make_async_copy(
            tiles_hbm.at[dd // 2, :, pl.ds(pl.multiple_of((dd % 2) * NCO, NCO), NCO), :],
            tl.at[n],
            tl_sem,
        )

    def start_tile(n, _):
        tile_load(n).start()
        return 0

    lax.fori_loop(0, NY * NX, start_tile, 0)

    small[0].wait()
    points = lax.broadcasted_iota(jnp.int32, (NCO, COLS), 0)
    onehot[...] = (points == co_ref[...]).astype(f32).astype(bf16)
    sums = [jnp.zeros((LEV, NCO), f32) for _ in range(4)]
    for i in range(steps):
        at = pl.ds(i * CH, CH)
        for a in loads[i]:
            a.wait()
        hot = onehot[:, at]
        for s in range(4):
            w = mem[s, :, at].astype(f32) * inc[s % 2, :, at].astype(f32)
            hi = w.astype(bf16)
            lo = (w - hi.astype(f32)).astype(bf16)
            sums[s] = sums[s] + (nt(hi, hot) + nt(lo, hot))
    small[1].wait()
    summed = jnp.concatenate(sums, axis=1)
    coarse = lax.dot_general(
        vert_ref[...], summed, (((1,), (0,)), ((), ())),
        precision=lax.Precision.HIGHEST, preferred_element_type=f32,
    )
    coarse = jnp.concatenate([coarse, jnp.zeros((NY * LG - LEV, 4 * NCO), f32)], axis=0).astype(bf16)
    for g in range(NY):
        for p in range(2):
            s1[g, p] = coarse[g * LG:(g + 1) * LG, p * 128:(p + 1) * 128]

    pl.semaphore_wait(barrier, len(greet))

    for yy in y_peers:
        pltpu.make_async_remote_copy(
            src_ref=s1.at[yy], dst_ref=r1.at[y], send_sem=y_send, recv_sem=y_recv,
            device_id=(dom(yy, x, z), e), device_id_type=MESH,
        ).start()
    r1[y] = s1[y]
    for i in range(1, NX):
        pl.semaphore_signal(ready, inc=1, device_id=(dom(y, (x + i) % NX, z), e), device_id_type=MESH)
    s3[...] = jnp.zeros_like(s3)
    arrived = r1.at[pl.ds(0, NY - 1)]
    pltpu.make_async_copy(arrived, arrived, y_recv).wait()

    for p in range(2):
        for j in range(NY // 2):
            lo, hi = halves(r1[2 * j, p], r1[2 * j + 1, p])
            s2[2 * p, j] = lo
            s2[2 * p + 1, j] = hi
    own = x * NZ + z
    pl.semaphore_wait(ready, NX - 1)
    for xx, zz in w_peers:
        pltpu.make_async_remote_copy(
            src_ref=s2.at[xx], dst_ref=r2.at[own], send_sem=w_send, recv_sem=w_recv,
            device_id=(dom(y, xx, zz), e), device_id_type=MESH,
        ).start()
    r2[own] = s2[x]
    for q in range(NZL):
        pltpu.make_async_remote_copy(
            src_ref=mem.at[:, :, pl.ds(pl.multiple_of((q * 2 + 1 - core) * OC, OC), OC)],
            dst_ref=pm.at[q], send_sem=pm_send.at[q], recv_sem=pm_recv.at[q],
            device_id=partner, device_id_type=MESH,
        ).start()
    arrived = r2.at[pl.ds(0, NX * NZ - 1)]
    pltpu.make_async_copy(arrived, arrived, w_recv).wait()

    for j in range(NY // 2):
        for v in range(NX * NZ // 2):
            lo, hi = halves(r2[2 * v, j], r2[2 * v + 1, j])
            blk[2 * j * (NX * NZ // 2) + v] = lo
            blk[(2 * j + 1) * (NX * NZ // 2) + v] = hi
    pltpu.make_async_copy(tl, tl, tl_sem).wait()
    small[2].wait()
    slot = x * NY + y
    for g in range(0, NY * NX, 8):
        group = b_peers[g:g + 8]
        for yy, xx in group:
            n = yy * NX + xx
            b = dom(yy, xx, z) // 2
            picked = jnp.concatenate([blk[cols_ref[t, b]] for t in range(NNZ)], axis=1)
            matrix = jnp.concatenate([tl[n, t] for t in range(NNZ)], axis=1)
            s3[n, :, :NCO] = nt(picked, matrix).astype(bf16)
        for yy, xx in group[:NY * NX - 1 - g]:
            pltpu.make_async_remote_copy(
                src_ref=s3.at[yy * NX + xx], dst_ref=r3.at[slot], send_sem=b_send, recv_sem=b_recv,
                device_id=(dom(yy, xx, z), e), device_id_type=MESH,
            ).start()
    r3[slot] = s3[y * NX + x]
    arrived = r3.at[pl.ds(0, NY * NX - 1)]
    pltpu.make_async_copy(arrived, arrived, b_recv).wait()

    swap = pltpu.make_async_remote_copy(
        src_ref=r3, dst_ref=pr3, send_sem=p_send, recv_sem=p_recv,
        device_id=partner, device_id_type=MESH,
    )
    swap.start()

    def term(s, fields, local, hot):
        lhs = local[s * NY:(s + 1) * NY].reshape(NY * LG, 128)[:, :NCO]
        back = jnp.dot(lhs, hot, preferred_element_type=f32)
        return fields.astype(f32) * back[:LEV]

    far = zl // 2
    targets = [3 * (1 - far), 2 - far, zl + 1 - 2 * (zl % 2), zl]
    kept = None
    for i, q in enumerate(targets):
        at = pl.ds(pl.multiple_of((q * 2 + core) * OC, OC), OC)
        hot = onehot[:, at]
        parts = [sum(term(k * 2 + c, mem[k * 2 + c, :, at], r3, hot) for k in range(2)) for c in range(2)]
        if i == 0:
            swap.wait_recv()
            for j in range(NZL):
                pltpu.make_async_copy(pm.at[j], pm.at[j], pm_recv.at[j]).wait()
        for c in range(2):
            parts[c] = parts[c] + sum(term(k * 2 + c, pm[q, k * 2 + c], pr3, hot) for k in range(2))
        both = jnp.concatenate(parts, axis=0)
        if i < NZL - 1:
            sc[i] = both.astype(bf16)
            pltpu.make_async_remote_copy(
                src_ref=sc.at[i], dst_ref=rb.at[zl], send_sem=c_send.at[i], recv_sem=c_recv.at[zl],
                device_id=(d, q * 2 + core), device_id_type=MESH,
            ).start()
        else:
            kept = both
    for i in (1, 3, 2):
        j = (zl + i) % NZL
        pltpu.make_async_copy(rb.at[j], rb.at[j], c_recv.at[j]).wait()
        kept = kept + rb[j].astype(f32)
    kept = (kept / 15.0).astype(bf16)
    out_ref[0] = kept[:LEV]
    out_ref[1] = kept[LEV:]

    for ref, count, sem in ((r1, NY - 1, y_send), (r2, NX * NZ - 1, w_send), (r3, NY * NX - 1, b_send)):
        sent = ref.at[pl.ds(0, count)]
        pltpu.make_async_copy(sent, sent, sem).wait()
    for q in range(NZL):
        pltpu.make_async_copy(pm.at[q], pm.at[q], pm_send.at[q]).wait()
    swap.wait_send()
    for i in range(NZL - 1):
        pltpu.make_async_copy(sc.at[i], sc.at[i], c_send.at[i]).wait()


def shards(members, increment, vert_loc, tiles, tile_cols, coarse_of):
    dma = pltpu.SemaphoreType.DMA
    vmem = pl.BlockSpec(memory_space=pltpu.VMEM)
    hbm = pl.BlockSpec(memory_space=pl.ANY)
    return pl.pallas_call(
        kernel,
        name="covary",
        out_shape=jax.ShapeDtypeStruct((2, LEV, OC), bf16),
        in_specs=[hbm] * 6,
        out_specs=vmem,
        scratch_shapes=[
            pltpu.VMEM((LEV, LEV), f32),
            pltpu.SMEM((NNZ, NY * NX * NZ // 2), jnp.int32),
            pltpu.VMEM((1, COLS), jnp.int32),
            pltpu.VMEM((4, LEV, COLS), bf16),
            pltpu.VMEM((2, LEV, COLS), bf16),
            pltpu.VMEM((NY * NX, NNZ, NCO, TILE), bf16),
            pltpu.VMEM((NCO, COLS), bf16),
            pltpu.VMEM((NY, 2, LG, 128), bf16),
            pltpu.VMEM((NY, 2, LG, 128), bf16),
            pltpu.VMEM((NX, NY // 2, LG, 128), bf16),
            pltpu.VMEM((NX * NZ, NY // 2, LG, 128), bf16),
            pltpu.VMEM((NY * NX * NZ // 2, LG, 128), bf16),
            pltpu.VMEM((NY * NX, LG, 128), bf16),
            pltpu.VMEM((NY * NX, LG, 128), bf16),
            pltpu.VMEM((NY * NX, LG, 128), bf16),
            pltpu.VMEM((NZL, 4, LEV, OC), bf16),
            pltpu.VMEM((NZL - 1, 2 * LEV, OC), bf16),
            pltpu.VMEM((NZL, 2 * LEV, OC), bf16),
            dma((3,)), dma((COLS // CH, 2)), dma,
            dma, dma, dma, dma, dma, dma,
            dma((NZL,)), dma((NZL,)), dma, dma, dma((NZL - 1,)), dma((NZL,)),
            pltpu.SemaphoreType.REGULAR,
        ],
        compiler_params=pltpu.CompilerParams(
            collective_id=0, has_side_effects=True, vmem_limit_bytes=63 * 2**20
        ),
    )(
        members.reshape(4, LEV, COLS), increment, vert_loc, tiles, tile_cols.T,
        coarse_of.reshape(1, COLS),
    )


def solution(mesh):
    return jax.shard_map(
        shards,
        mesh=mesh,
        in_specs=(P("ens", None, None, "dom"), P(None, None, "dom"), P(), P(), P(), P("dom")),
        out_specs=P(None, None, ("dom", "ens")),
        check_vma=False,
    )
```

```python
import jax
import jax.numpy as jnp
from jax import lax
from jax.experimental import pallas as pl
from jax.experimental.pallas import tpu as pltpu
from jax.sharding import PartitionSpec as P

MESH = pl.DeviceIdType.MESH
NY, NX, NZ = 8, 4, 3
NZL = 4
LEV, COLS, NCO = 120, 2048, 64
LG = 16
TILE, NNZ = 128, 4
CH = 512
OC = 256
bf16, f32 = jnp.bfloat16, jnp.float32


def nt(a, b):
    return lax.dot_general(a, b, (((1,), (1,)), ((), ())), preferred_element_type=f32)


def halves(a, b):
    lo = jnp.concatenate([a[:, :NCO], b[:, :NCO]], axis=1)
    hi = jnp.concatenate([a[:, NCO:], b[:, NCO:]], axis=1)
    return lo, hi


def kernel(
    mem_hbm, inc_hbm, vert_hbm, tiles_hbm, cols_hbm, co_hbm, out_ref,
    vert_ref, cols_ref, co_ref, mem, inc, tl, onehot, s1, r1, s2, r2, blk, s3, r3, pr3, pm, sc, rb,
    small_sem, in_sem, tl_sem, y_send, y_recv, w_send, w_recv, b_send, b_recv,
    pm_send, pm_recv, p_send, p_recv, c_send, c_recv, ready,
):
    d = lax.axis_index("dom")
    e = lax.axis_index("ens")
    y, x, z = d // (NX * NZ), (d // NZ) % NX, d % NZ
    zl, core = e // 2, e % 2

    def dom(yy, xx, zz):
        return (yy * NX + xx) * NZ + zz

    partner = (d, zl * 2 + 1 - core)
    y_peers = [(y + i) % NY for i in (4, 3, 5, 2, 6, 1, 7)]
    w_peers = [((x + i) % NX, (z + k) % NZ) for i in (2, 1, 3, 0) for k in (1, 2, 0) if i or k]
    b_peers = [((y + i) % NY, (x + k) % NX) for i in (4, 3, 5, 2, 6, 1, 7, 0) for k in (2, 1, 3, 0)]

    small = [
        pltpu.make_async_copy(src, dst, small_sem.at[i])
        for i, (src, dst) in enumerate(((co_hbm, co_ref), (vert_hbm, vert_ref), (cols_hbm, cols_ref)))
    ]
    for copy in small:
        copy.start()
    steps = COLS // CH
    loads = []
    for i in range(steps):
        at = pl.ds(i * CH, CH)
        a = pltpu.make_async_copy(mem_hbm.at[:, :, at], mem.at[:, :, at], in_sem.at[i, 0])
        b = pltpu.make_async_copy(inc_hbm.at[:, :, at], inc.at[:, :, at], in_sem.at[i, 1])
        a.start()
        b.start()
        loads.append((a, b))

    barrier = pltpu.get_barrier_semaphore()
    greet = [(dom(yy, x, z), e) for yy in y_peers]
    greet += [(dom(y, (x + i) % NX, z), e) for i in range(1, NX)]
    greet += [(dom(y, x, (z + i) % NZ), e) for i in range(1, NZ)]
    greet += [(d, ((zl + i) % NZL) * 2 + core) for i in range(1, NZL)]
    greet += [partner]
    for peer in greet:
        pl.semaphore_signal(barrier, inc=1, device_id=peer, device_id_type=MESH)

    def tile_load(n):
        dd = dom(n // NX, n % NX, z)
        return pltpu.make_async_copy(
            tiles_hbm.at[dd // 2, :, pl.ds(pl.multiple_of((dd % 2) * NCO, NCO), NCO), :],
            tl.at[n],
            tl_sem,
        )

    def start_tile(n, _):
        tile_load(n).start()
        return 0

    lax.fori_loop(0, NY * NX, start_tile, 0)

    small[0].wait()
    points = lax.broadcasted_iota(jnp.int32, (NCO, COLS), 0)
    onehot[...] = (points == co_ref[...]).astype(f32).astype(bf16)
    sums = [jnp.zeros((LEV, NCO), f32) for _ in range(4)]
    for i in range(steps):
        at = pl.ds(i * CH, CH)
        for a in loads[i]:
            a.wait()
        hot = onehot[:, at]
        for s in range(4):
            w = mem[s, :, at].astype(f32) * inc[s % 2, :, at].astype(f32)
            hi = w.astype(bf16)
            lo = (w - hi.astype(f32)).astype(bf16)
            sums[s] = sums[s] + (nt(hi, hot) + nt(lo, hot))
    small[1].wait()
    summed = jnp.concatenate(sums, axis=1)
    coarse = lax.dot_general(
        vert_ref[...], summed, (((1,), (0,)), ((), ())),
        precision=lax.Precision.HIGHEST, preferred_element_type=f32,
    )
    coarse = jnp.concatenate([coarse, jnp.zeros((NY * LG - LEV, 4 * NCO), f32)], axis=0).astype(bf16)
    for g in range(NY):
        for p in range(2):
            s1[g, p] = coarse[g * LG:(g + 1) * LG, p * 128:(p + 1) * 128]

    pl.semaphore_wait(barrier, len(greet))

    for yy in y_peers:
        pltpu.make_async_remote_copy(
            src_ref=s1.at[yy], dst_ref=r1.at[y], send_sem=y_send, recv_sem=y_recv,
            device_id=(dom(yy, x, z), e), device_id_type=MESH,
        ).start()
    r1[y] = s1[y]
    for i in range(1, NX):
        pl.semaphore_signal(ready, inc=1, device_id=(dom(y, (x + i) % NX, z), e), device_id_type=MESH)
    arrived = r1.at[pl.ds(0, NY - 1)]
    pltpu.make_async_copy(arrived, arrived, y_recv).wait()

    def sent_to(zz):
        @pl.when(z != zz)
        def _():
            sent = r2.at[pl.ds(0, NX)]
            pltpu.make_async_copy(sent, sent, w_send.at[zz]).wait()

        @pl.when(z == zz)
        def _():
            sent = r2.at[pl.ds(0, NX - 1)]
            pltpu.make_async_copy(sent, sent, w_send.at[zz]).wait()

    for p in range(2):
        for j in range(NY // 2):
            lo, hi = halves(r1[2 * j, p], r1[2 * j + 1, p])
            s2[2 * p, j] = lo
            s2[2 * p + 1, j] = hi
    own = x * NZ + z
    pl.semaphore_wait(ready, NX - 1)
    for zz in range(NZ):
        for i in (2, 1, 3, 0):
            xx = (x + i) % NX
            copy = pltpu.make_async_remote_copy(
                src_ref=s2.at[xx], dst_ref=r2.at[own], send_sem=w_send.at[zz], recv_sem=w_recv,
                device_id=(dom(y, xx, zz), e), device_id_type=MESH,
            )
            if i:
                copy.start()
            else:
                pl.when(z != zz)(copy.start)
        if zz == 0:
            sent_to(zz)
    r2[own] = s2[x]
    for q in range(NZL):
        pltpu.make_async_remote_copy(
            src_ref=mem.at[:, :, pl.ds(pl.multiple_of((q * 2 + 1 - core) * OC, OC), OC)],
            dst_ref=pm.at[q], send_sem=pm_send.at[q], recv_sem=pm_recv.at[q],
            device_id=partner, device_id_type=MESH,
        ).start()
    arrived = r2.at[pl.ds(0, NX * NZ - 1)]
    pltpu.make_async_copy(arrived, arrived, w_recv).wait()

    for j in range(NY // 2):
        for v in range(NX * NZ // 2):
            lo, hi = halves(r2[2 * v, j], r2[2 * v + 1, j])
            blk[2 * j * (NX * NZ // 2) + v] = lo
            blk[(2 * j + 1) * (NX * NZ // 2) + v] = hi
    pltpu.make_async_copy(tl, tl, tl_sem).wait()
    small[2].wait()
    slot = x * NY + y
    for g in range(0, NY * NX, 8):
        group = b_peers[g:g + 8]
        for yy, xx in group:
            n = yy * NX + xx
            b = dom(yy, xx, z) // 2
            picked = jnp.concatenate([blk[cols_ref[t, b]] for t in range(NNZ)], axis=1)
            matrix = jnp.concatenate([tl[n, t] for t in range(NNZ)], axis=1)
            smooth = nt(picked, matrix)
            s3[n] = jnp.concatenate([smooth[:LG // 2], smooth[LG // 2:]], axis=1).astype(bf16)
        for peer in group:
            yy, xx = peer
            if peer is not b_peers[-1]:
                pltpu.make_async_remote_copy(
                    src_ref=s3.at[yy * NX + xx], dst_ref=r3.at[slot], send_sem=b_send, recv_sem=b_recv,
                    device_id=(dom(yy, xx, z), e), device_id_type=MESH,
                ).start()
            pltpu.make_async_remote_copy(
                src_ref=s3.at[yy * NX + xx], dst_ref=pr3.at[slot], send_sem=p_send, recv_sem=p_recv,
                device_id=(dom(yy, xx, z), zl * 2 + 1 - core), device_id_type=MESH,
            ).start()
    r3[slot] = s3[y * NX + x]
    arrived = r3.at[pl.ds(0, NY * NX - 1)]
    pltpu.make_async_copy(arrived, arrived, b_recv).wait()
    pltpu.make_async_copy(pr3, pr3, p_recv).wait()
    for j in range(NZL):
        pltpu.make_async_copy(pm.at[j], pm.at[j], pm_recv.at[j]).wait()

    def rows(field):
        tiles = [field[g * 8:(g + 1) * 8] for g in range(LEV // 8)]
        return jnp.concatenate(tiles[0::2] + tiles[1::2], axis=0)

    def packed(ref, s):
        return ref[s * NY:(s + 1) * NY].astype(f32).reshape(NY * LG // 2, 128).astype(bf16)

    local = [packed(r3, s) for s in range(4)] + [packed(pr3, s) for s in range(4)]
    none = jnp.zeros((NCO, OC), bf16)

    def term(s, field, hot):
        back = [jnp.dot(local[s], h, preferred_element_type=f32) for h in hot]
        return rows(field.astype(f32)) * jnp.concatenate(back, axis=0)[:LEV]

    far = zl // 2
    targets = [3 * (1 - far), 2 - far, zl + 1 - 2 * (zl % 2), zl]
    kept = None
    for i, q in enumerate(targets):
        at = pl.ds(pl.multiple_of((q * 2 + core) * OC, OC), OC)
        hot = onehot[:, at]
        hot = jnp.concatenate([hot, none], axis=0), jnp.concatenate([none, hot], axis=0)
        parts = [
            sum(term(k * 2 + c, mem[k * 2 + c, :, at], hot) for k in range(2))
            + sum(term(4 + k * 2 + c, pm[q, k * 2 + c], hot) for k in range(2))
            for c in range(2)
        ]
        both = jnp.concatenate(parts, axis=0)
        if i < NZL - 1:
            sc[i] = both.astype(bf16)
            pltpu.make_async_remote_copy(
                src_ref=sc.at[i], dst_ref=rb.at[zl], send_sem=c_send.at[i], recv_sem=c_recv.at[zl],
                device_id=(d, q * 2 + core), device_id_type=MESH,
            ).start()
        else:
            kept = both
    for i in (1, 3, 2):
        j = (zl + i) % NZL
        pltpu.make_async_copy(rb.at[j], rb.at[j], c_recv.at[j]).wait()
        kept = kept + rb[j].astype(f32)
    kept = kept / 15.0
    for c in range(2):
        tiles = [kept[c * LEV + g * 8:c * LEV + (g + 1) * 8] for g in range(LEV // 8)]
        first = (LEV // 8 + 1) // 2
        order = [tiles[g // 2 + first * (g % 2)] for g in range(LEV // 8)]
        out_ref[c] = jnp.concatenate(order, axis=0).astype(bf16)

    for ref, count, sem in ((r1, NY - 1, y_send), (r3, NY * NX - 1, b_send)):
        sent = ref.at[pl.ds(0, count)]
        pltpu.make_async_copy(sent, sent, sem).wait()
    for zz in range(1, NZ):
        sent_to(zz)
    for q in range(NZL):
        pltpu.make_async_copy(pm.at[q], pm.at[q], pm_send.at[q]).wait()
    pltpu.make_async_copy(pr3, pr3, p_send).wait()
    for i in range(NZL - 1):
        pltpu.make_async_copy(sc.at[i], sc.at[i], c_send.at[i]).wait()


def shards(members, increment, vert_loc, tiles, tile_cols, coarse_of):
    dma = pltpu.SemaphoreType.DMA
    vmem = pl.BlockSpec(memory_space=pltpu.VMEM)
    hbm = pl.BlockSpec(memory_space=pl.ANY)
    return pl.pallas_call(
        kernel,
        name="covary",
        out_shape=jax.ShapeDtypeStruct((2, LEV, OC), bf16),
        in_specs=[hbm] * 6,
        out_specs=vmem,
        scratch_shapes=[
            pltpu.VMEM((LEV, LEV), f32),
            pltpu.SMEM((NNZ, NY * NX * NZ // 2), jnp.int32),
            pltpu.VMEM((1, COLS), jnp.int32),
            pltpu.VMEM((4, LEV, COLS), bf16),
            pltpu.VMEM((2, LEV, COLS), bf16),
            pltpu.VMEM((NY * NX, NNZ, NCO, TILE), bf16),
            pltpu.VMEM((NCO, COLS), bf16),
            pltpu.VMEM((NY, 2, LG, 128), bf16),
            pltpu.VMEM((NY, 2, LG, 128), bf16),
            pltpu.VMEM((NX, NY // 2, LG, 128), bf16),
            pltpu.VMEM((NX * NZ, NY // 2, LG, 128), bf16),
            pltpu.VMEM((NY * NX * NZ // 2, LG, 128), bf16),
            pltpu.VMEM((NY * NX, LG // 2, 128), bf16),
            pltpu.VMEM((NY * NX, LG // 2, 128), bf16),
            pltpu.VMEM((NY * NX, LG // 2, 128), bf16),
            pltpu.VMEM((NZL, 4, LEV, OC), bf16),
            pltpu.VMEM((NZL - 1, 2 * LEV, OC), bf16),
            pltpu.VMEM((NZL, 2 * LEV, OC), bf16),
            dma((3,)), dma((COLS // CH, 2)), dma,
            dma, dma, dma((NZ,)), dma, dma, dma,
            dma((NZL,)), dma((NZL,)), dma, dma, dma((NZL - 1,)), dma((NZL,)),
            pltpu.SemaphoreType.REGULAR,
        ],
        compiler_params=pltpu.CompilerParams(
            collective_id=0, has_side_effects=True, vmem_limit_bytes=63 * 2**20
        ),
    )(
        members.reshape(4, LEV, COLS), increment, vert_loc, tiles, tile_cols.T,
        coarse_of.reshape(1, COLS),
    )


def solution(mesh):
    return jax.shard_map(
        shards,
        mesh=mesh,
        in_specs=(P("ens", None, None, "dom"), P(None, None, "dom"), P(), P(), P(), P("dom")),
        out_specs=P(None, None, ("dom", "ens")),
        check_vma=False,
    )
```

```python
import jax
import jax.numpy as jnp
from jax import lax
from jax.experimental import pallas as pl
from jax.experimental.pallas import tpu as pltpu
from jax.sharding import PartitionSpec as P

MESH = pl.DeviceIdType.MESH
NY, NX, NZ = 8, 4, 3
NZL = 4
LEV, COLS, NCO = 120, 2048, 64
LG = 16
TILE, NNZ = 128, 4
CH = 512
OC = 256
bf16, f32 = jnp.bfloat16, jnp.float32


def nt(a, b):
    return lax.dot_general(a, b, (((1,), (1,)), ((), ())), preferred_element_type=f32)


def halves(a, b):
    lo = jnp.concatenate([a[:, :NCO], b[:, :NCO]], axis=1)
    hi = jnp.concatenate([a[:, NCO:], b[:, NCO:]], axis=1)
    return lo, hi


def kernel(
    mem_hbm, inc_hbm, vert_hbm, tiles_hbm, cols_hbm, co_hbm, out_ref,
    vert_ref, cols_ref, co_ref, mem, inc, tl, onehot, s1, ra, blk, s3, r3, pr3, pm, sc, rb,
    small_sem, in_sem, tl_sem, a_send, d_send, a_recv, z_send, b_send, b_recv,
    pm_send, pm_recv, p_send, p_recv, c_send, c_recv, ready,
):
    d = lax.axis_index("dom")
    e = lax.axis_index("ens")
    y, x, z = d // (NX * NZ), (d // NZ) % NX, d % NZ
    zl, core = e // 2, e % 2

    def dom(yy, xx, zz):
        return (yy * NX + xx) * NZ + zz

    partner = (d, zl * 2 + 1 - core)
    peers = [((y + i) % NY, (x + k) % NX) for i in (4, 3, 5, 2, 6, 1, 7, 0) for k in (2, 1, 3, 0)]
    lines = [((y + i) % NY, x) for i in (4, 3, 5, 2, 6, 1, 7)] + [(y, (x + k) % NX) for k in (2, 1, 3)]
    rest = [((y + i) % NY, (x + k) % NX) for i in (4, 3, 5, 2, 6, 1, 7) for k in (2, 1, 3)]
    me = y * NX + x

    small = [
        pltpu.make_async_copy(src, dst, small_sem.at[i])
        for i, (src, dst) in enumerate(((co_hbm, co_ref), (vert_hbm, vert_ref), (cols_hbm, cols_ref)))
    ]
    for copy in small:
        copy.start()
    steps = COLS // CH
    loads = []
    for i in range(steps):
        at = pl.ds(i * CH, CH)
        a = pltpu.make_async_copy(mem_hbm.at[:, :, at], mem.at[:, :, at], in_sem.at[i, 0])
        b = pltpu.make_async_copy(inc_hbm.at[:, :, at], inc.at[:, :, at], in_sem.at[i, 1])
        a.start()
        b.start()
        loads.append((a, b))

    barrier = pltpu.get_barrier_semaphore()

    def greet(peer):
        pl.semaphore_signal(barrier, inc=1, device_id=peer, device_id_type=MESH)

    @pl.when(z == 0)
    def _():
        for yy, xx in peers:
            for zz in range(1, NZ):
                greet((dom(yy, xx, zz), e))

    for yy, xx in lines:
        greet((dom(yy, xx, z), e))
    for i in range(1, NZL):
        greet((d, ((zl + i) % NZL) * 2 + core))
    greet(partner)

    @pl.when(z != 0)
    def _():
        greet((dom(y, x, 0), e))
        greet((dom(y, x, NZ - z), e))

    small[0].wait()
    points = lax.broadcasted_iota(jnp.int32, (NCO, COLS), 0)
    onehot[...] = (points == co_ref[...]).astype(f32).astype(bf16)
    sums = [jnp.zeros((LEV, NCO), f32) for _ in range(4)]
    for i in range(steps):
        at = pl.ds(i * CH, CH)
        for a in loads[i]:
            a.wait()
        hot = onehot[:, at]
        for s in range(4):
            w = mem[s, :, at].astype(f32) * inc[s % 2, :, at].astype(f32)
            hi = w.astype(bf16)
            lo = (w - hi.astype(f32)).astype(bf16)
            sums[s] = sums[s] + (nt(hi, hot) + nt(lo, hot))
    small[1].wait()
    summed = jnp.concatenate(sums, axis=1)
    coarse = lax.dot_general(
        vert_ref[...], summed, (((1,), (0,)), ((), ())),
        precision=lax.Precision.HIGHEST, preferred_element_type=f32,
    )
    coarse = jnp.concatenate([coarse, jnp.zeros((NY * LG - LEV, 4 * NCO), f32)], axis=0)
    for g in range(NY):
        for s in range(NX):
            part = coarse[g * LG:(g + 1) * LG, s * NCO:(s + 1) * NCO]
            s1[g * NX + s] = jnp.concatenate([part[:LG // 2], part[LG // 2:]], axis=1).astype(bf16)

    here = len(lines) + NZL

    @pl.when(z == 0)
    def _():
        pl.semaphore_wait(barrier, here + NZ - 1)

    def deal(yy, xx, zz, sem):
        pltpu.make_async_remote_copy(
            src_ref=s1.at[yy * NX + xx], dst_ref=ra.at[z, me], send_sem=sem, recv_sem=a_recv.at[z],
            device_id=(dom(yy, xx, zz), e), device_id_type=MESH,
        ).start()

    @pl.when(z != 0)
    def _():
        pl.semaphore_wait(barrier, here + NY * NX + 1)
        for yy, xx in peers:
            deal(yy, xx, 0, d_send)

    for xx in [(x + k) % NX for k in (2, 1, 3)]:
        pl.semaphore_signal(ready, inc=1, device_id=(dom(y, xx, z), e), device_id_type=MESH)
    for yy, xx in lines:
        deal(yy, xx, z, a_send)
    ra[z, me] = s1[me]
    pl.semaphore_wait(ready, NX - 1)
    for yy, xx in rest:
        deal(yy, xx, z, a_send)
    for q in range(NZL):
        pltpu.make_async_remote_copy(
            src_ref=mem.at[:, :, pl.ds(pl.multiple_of((q * 2 + 1 - core) * OC, OC), OC)],
            dst_ref=pm.at[q], send_sem=pm_send.at[q], recv_sem=pm_recv.at[q],
            device_id=partner, device_id_type=MESH,
        ).start()
    def tile_load(n):
        dd = dom(n // NX, n % NX, z)
        return pltpu.make_async_copy(
            tiles_hbm.at[dd // 2, :, pl.ds(pl.multiple_of((dd % 2) * NCO, NCO), NCO), :],
            tl.at[n],
            tl_sem,
        )

    def start_tile(n, _):
        tile_load(n).start()
        return 0

    lax.fori_loop(0, NY * NX, start_tile, 0)

    arrived = ra.at[z, pl.ds(0, NY * NX - 1)]
    pltpu.make_async_copy(arrived, arrived, a_recv.at[z]).wait()

    def along(zz, i):
        return pltpu.make_async_remote_copy(
            src_ref=ra.at[z], dst_ref=ra.at[z], send_sem=z_send.at[i], recv_sem=a_recv.at[z],
            device_id=(dom(y, x, zz), e), device_id_type=MESH,
        )

    along(NZ - 1 - z // 2, 0).start()
    pl.when(z == 0)(along(1, 1).start)
    for i in (1, 2):
        zz = (z + i) % NZ
        pltpu.make_async_copy(ra.at[zz], ra.at[zz], a_recv.at[zz]).wait()

    for b in range(NY * NX * NZ // 2):
        pair = [ra[dd % NZ, dd // NZ].astype(f32) for dd in (2 * b, 2 * b + 1)]
        blk[b] = jnp.concatenate(halves(*pair), axis=0).astype(bf16)
    pltpu.make_async_copy(tl, tl, tl_sem).wait()
    small[2].wait()
    slot = x * NY + y
    for g in range(0, NY * NX, 8):
        group = peers[g:g + 8]
        for yy, xx in group:
            n = yy * NX + xx
            b = dom(yy, xx, z) // 2
            picked = jnp.concatenate([blk[cols_ref[t, b]] for t in range(NNZ)], axis=1)
            matrix = jnp.concatenate([tl[n, t] for t in range(NNZ)], axis=1)
            smooth = nt(picked, matrix)
            s3[n] = jnp.concatenate([smooth[:LG // 2], smooth[LG // 2:]], axis=1).astype(bf16)
        for peer in group:
            yy, xx = peer
            if peer is not peers[-1]:
                pltpu.make_async_remote_copy(
                    src_ref=s3.at[yy * NX + xx], dst_ref=r3.at[slot], send_sem=b_send, recv_sem=b_recv,
                    device_id=(dom(yy, xx, z), e), device_id_type=MESH,
                ).start()
            pltpu.make_async_remote_copy(
                src_ref=s3.at[yy * NX + xx], dst_ref=pr3.at[slot], send_sem=p_send, recv_sem=p_recv,
                device_id=(dom(yy, xx, z), zl * 2 + 1 - core), device_id_type=MESH,
            ).start()
    r3[slot] = s3[y * NX + x]
    arrived = r3.at[pl.ds(0, NY * NX - 1)]
    pltpu.make_async_copy(arrived, arrived, b_recv).wait()
    pltpu.make_async_copy(pr3, pr3, p_recv).wait()
    for j in range(NZL):
        pltpu.make_async_copy(pm.at[j], pm.at[j], pm_recv.at[j]).wait()

    def rows(field):
        tiles = [field[g * 8:(g + 1) * 8] for g in range(LEV // 8)]
        return jnp.concatenate(tiles[0::2] + tiles[1::2], axis=0)

    def packed(ref, s):
        return ref[s * NY:(s + 1) * NY].astype(f32).reshape(NY * LG // 2, 128).astype(bf16)

    local = [packed(r3, s) for s in range(4)] + [packed(pr3, s) for s in range(4)]
    none = jnp.zeros((NCO, OC), bf16)

    def term(s, field, hot):
        back = [jnp.dot(local[s], h, preferred_element_type=f32) for h in hot]
        return rows(field.astype(f32)) * jnp.concatenate(back, axis=0)[:LEV]

    far = zl // 2
    targets = [3 * (1 - far), 2 - far, zl + 1 - 2 * (zl % 2), zl]
    kept = None
    for i, q in enumerate(targets):
        at = pl.ds(pl.multiple_of((q * 2 + core) * OC, OC), OC)
        hot = onehot[:, at]
        hot = jnp.concatenate([hot, none], axis=0), jnp.concatenate([none, hot], axis=0)
        parts = [
            sum(term(k * 2 + c, mem[k * 2 + c, :, at], hot) for k in range(2))
            + sum(term(4 + k * 2 + c, pm[q, k * 2 + c], hot) for k in range(2))
            for c in range(2)
        ]
        both = jnp.concatenate(parts, axis=0)
        if i < NZL - 1:
            sc[i] = both.astype(bf16)
            pltpu.make_async_remote_copy(
                src_ref=sc.at[i], dst_ref=rb.at[zl], send_sem=c_send.at[i], recv_sem=c_recv.at[zl],
                device_id=(d, q * 2 + core), device_id_type=MESH,
            ).start()
        else:
            kept = both
    for i in (1, 3, 2):
        j = (zl + i) % NZL
        pltpu.make_async_copy(rb.at[j], rb.at[j], c_recv.at[j]).wait()
        kept = kept + rb[j].astype(f32)
    kept = kept / 15.0
    for c in range(2):
        tiles = [kept[c * LEV + g * 8:c * LEV + (g + 1) * 8] for g in range(LEV // 8)]
        first = (LEV // 8 + 1) // 2
        order = [tiles[g // 2 + first * (g % 2)] for g in range(LEV // 8)]
        out_ref[c] = jnp.concatenate(order, axis=0).astype(bf16)

    for ref, sem in ((r3, a_send), (r3, b_send)):
        sent = ref.at[pl.ds(0, NY * NX - 1)]
        pltpu.make_async_copy(sent, sent, sem).wait()
    pltpu.make_async_copy(ra.at[0], ra.at[0], z_send.at[0]).wait()

    @pl.when(z == 0)
    def _():
        pltpu.make_async_copy(ra.at[0], ra.at[0], z_send.at[1]).wait()

    @pl.when(z != 0)
    def _():
        pltpu.make_async_copy(ra.at[0], ra.at[0], d_send).wait()

    for q in range(NZL):
        pltpu.make_async_copy(pm.at[q], pm.at[q], pm_send.at[q]).wait()
    pltpu.make_async_copy(pr3, pr3, p_send).wait()
    for i in range(NZL - 1):
        pltpu.make_async_copy(sc.at[i], sc.at[i], c_send.at[i]).wait()


def shards(members, increment, vert_loc, tiles, tile_cols, coarse_of):
    dma = pltpu.SemaphoreType.DMA
    vmem = pl.BlockSpec(memory_space=pltpu.VMEM)
    hbm = pl.BlockSpec(memory_space=pl.ANY)
    return pl.pallas_call(
        kernel,
        name="covary",
        out_shape=jax.ShapeDtypeStruct((2, LEV, OC), bf16),
        in_specs=[hbm] * 6,
        out_specs=vmem,
        scratch_shapes=[
            pltpu.VMEM((LEV, LEV), f32),
            pltpu.SMEM((NNZ, NY * NX * NZ // 2), jnp.int32),
            pltpu.VMEM((1, COLS), jnp.int32),
            pltpu.VMEM((4, LEV, COLS), bf16),
            pltpu.VMEM((2, LEV, COLS), bf16),
            pltpu.VMEM((NY * NX, NNZ, NCO, TILE), bf16),
            pltpu.VMEM((NCO, COLS), bf16),
            pltpu.VMEM((NY * NX, LG // 2, 128), bf16),
            pltpu.VMEM((NZ, NY * NX, LG // 2, 128), bf16),
            pltpu.VMEM((NY * NX * NZ // 2, LG, 128), bf16),
            pltpu.VMEM((NY * NX, LG // 2, 128), bf16),
            pltpu.VMEM((NY * NX, LG // 2, 128), bf16),
            pltpu.VMEM((NY * NX, LG // 2, 128), bf16),
            pltpu.VMEM((NZL, 4, LEV, OC), bf16),
            pltpu.VMEM((NZL - 1, 2 * LEV, OC), bf16),
            pltpu.VMEM((NZL, 2 * LEV, OC), bf16),
            dma((3,)), dma((COLS // CH, 2)), dma,
            dma, dma, dma((NZ,)), dma((2,)), dma, dma,
            dma((NZL,)), dma((NZL,)), dma, dma, dma((NZL - 1,)), dma((NZL,)),
            pltpu.SemaphoreType.REGULAR,
        ],
        compiler_params=pltpu.CompilerParams(
            collective_id=0, has_side_effects=True, vmem_limit_bytes=63 * 2**20
        ),
    )(
        members.reshape(4, LEV, COLS), increment, vert_loc, tiles, tile_cols.T,
        coarse_of.reshape(1, COLS),
    )


def solution(mesh):
    return jax.shard_map(
        shards,
        mesh=mesh,
        in_specs=(P("ens", None, None, "dom"), P(None, None, "dom"), P(), P(), P(), P("dom")),
        out_specs=P(None, None, ("dom", "ens")),
        check_vma=False,
    )
```

```python
import jax
import jax.numpy as jnp
from jax import lax
from jax.experimental import pallas as pl
from jax.experimental.pallas import tpu as pltpu
from jax.sharding import PartitionSpec as P

MESH = pl.DeviceIdType.MESH
NY, NX, NZ = 8, 4, 3
NZL = 4
LEV, COLS, NCO = 120, 2048, 64
LG = 16
TILE, NNZ = 128, 4
CH = 512
OC = 256
bf16, f32 = jnp.bfloat16, jnp.float32


def nt(a, b):
    return lax.dot_general(a, b, (((1,), (1,)), ((), ())), preferred_element_type=f32)


def halves(a, b):
    lo = jnp.concatenate([a[:, :NCO], b[:, :NCO]], axis=1)
    hi = jnp.concatenate([a[:, NCO:], b[:, NCO:]], axis=1)
    return lo, hi


def kernel(
    mem_hbm, inc_hbm, vert_hbm, tiles_hbm, cols_hbm, co_hbm, out_ref,
    vert_ref, cols_ref, co_ref, mem, inc, tl, onehot, s1, ra, blk, s3, r3, pr3, pm, sc, rb,
    small_sem, in_sem, tl_sem, a_send, d_send, a_recv, z_send, b_send, b_recv,
    pm_send, pm_recv, p_send, p_recv, c_send, c_recv, ready,
):
    d = lax.axis_index("dom")
    e = lax.axis_index("ens")
    y, x, z = d // (NX * NZ), (d // NZ) % NX, d % NZ
    zl, core = e // 2, e % 2

    def dom(yy, xx, zz):
        return (yy * NX + xx) * NZ + zz

    partner = (d, zl * 2 + 1 - core)
    peers = [((y + i) % NY, (x + k) % NX) for i in (4, 3, 5, 2, 6, 1, 7, 0) for k in (2, 1, 3, 0)]
    lines = [((y + i) % NY, x) for i in (4, 3, 5, 2, 6, 1, 7)] + [(y, (x + k) % NX) for k in (2, 1, 3)]
    rest = [((y + i) % NY, (x + k) % NX) for i in (4, 3, 5, 2, 6, 1, 7) for k in (2, 1, 3)]
    me = y * NX + x

    small = [
        pltpu.make_async_copy(src, dst, small_sem.at[i])
        for i, (src, dst) in enumerate(((co_hbm, co_ref), (vert_hbm, vert_ref), (cols_hbm, cols_ref)))
    ]
    for copy in small:
        copy.start()
    steps = COLS // CH
    loads = []
    for i in range(steps):
        at = pl.ds(i * CH, CH)
        a = pltpu.make_async_copy(mem_hbm.at[:, :, at], mem.at[:, :, at], in_sem.at[i, 0])
        b = pltpu.make_async_copy(inc_hbm.at[:, :, at], inc.at[:, :, at], in_sem.at[i, 1])
        a.start()
        b.start()
        loads.append((a, b))

    barrier = pltpu.get_barrier_semaphore()

    def greet(peer):
        pl.semaphore_signal(barrier, inc=1, device_id=peer, device_id_type=MESH)

    @pl.when(z == 0)
    def _():
        for yy, xx in peers:
            for zz in range(1, NZ):
                greet((dom(yy, xx, zz), e))

    for yy, xx in lines:
        greet((dom(yy, xx, z), e))
    for i in range(1, NZL):
        greet((d, ((zl + i) % NZL) * 2 + core))
    greet(partner)

    @pl.when(z != 0)
    def _():
        greet((dom(y, x, 0), e))
        greet((dom(y, x, NZ - z), e))

    small[0].wait()
    points = lax.broadcasted_iota(jnp.int32, (NCO, COLS), 0)
    onehot[...] = (points == co_ref[...]).astype(f32).astype(bf16)
    sums = [jnp.zeros((LEV, NCO), f32) for _ in range(4)]
    for i in range(steps):
        at = pl.ds(i * CH, CH)
        for a in loads[i]:
            a.wait()
        hot = onehot[:, at]
        for s in range(4):
            w = mem[s, :, at].astype(f32) * inc[s % 2, :, at].astype(f32)
            hi = w.astype(bf16)
            lo = (w - hi.astype(f32)).astype(bf16)
            sums[s] = sums[s] + (nt(hi, hot) + nt(lo, hot))
    small[1].wait()
    summed = jnp.concatenate(sums, axis=1)
    coarse = lax.dot_general(
        vert_ref[...], summed, (((1,), (0,)), ((), ())),
        precision=lax.Precision.HIGHEST, preferred_element_type=f32,
    )
    coarse = jnp.concatenate([coarse, jnp.zeros((NY * LG - LEV, 4 * NCO), f32)], axis=0)
    for g in range(NY):
        for s in range(NX):
            part = coarse[g * LG:(g + 1) * LG, s * NCO:(s + 1) * NCO]
            s1[g * NX + s] = jnp.concatenate([part[:LG // 2], part[LG // 2:]], axis=1).astype(bf16)

    here = len(lines) + NZL

    @pl.when(z == 0)
    def _():
        pl.semaphore_wait(barrier, here + NZ - 1)

    def deal(yy, xx, zz, sem):
        pltpu.make_async_remote_copy(
            src_ref=s1.at[yy * NX + xx], dst_ref=ra.at[z, me], send_sem=sem, recv_sem=a_recv.at[z],
            device_id=(dom(yy, xx, zz), e), device_id_type=MESH,
        ).start()

    @pl.when(z != 0)
    def _():
        pl.semaphore_wait(barrier, here + NY * NX + 1)
        for yy, xx in peers:
            deal(yy, xx, 0, d_send)

    for xx in [(x + k) % NX for k in (2, 1, 3)]:
        pl.semaphore_signal(ready, inc=1, device_id=(dom(y, xx, z), e), device_id_type=MESH)
    for yy, xx in lines:
        deal(yy, xx, z, a_send)
    ra[z, me] = s1[me]
    pl.semaphore_wait(ready, NX - 1)
    for yy, xx in rest:
        deal(yy, xx, z, a_send)
    for q in range(NZL):
        pltpu.make_async_remote_copy(
            src_ref=mem.at[:, :, pl.ds(pl.multiple_of((q * 2 + 1 - core) * OC, OC), OC)],
            dst_ref=pm.at[q], send_sem=pm_send.at[q], recv_sem=pm_recv.at[q],
            device_id=partner, device_id_type=MESH,
        ).start()
    def tile_load(n):
        dd = dom(n // NX, n % NX, z)
        return pltpu.make_async_copy(
            tiles_hbm.at[dd // 2, :, pl.ds(pl.multiple_of((dd % 2) * NCO, NCO), NCO), :],
            tl.at[n],
            tl_sem,
        )

    def start_tile(n, _):
        tile_load(n).start()
        return 0

    lax.fori_loop(0, NY * NX, start_tile, 0)

    arrived = ra.at[z, pl.ds(0, NY * NX - 1)]
    pltpu.make_async_copy(arrived, arrived, a_recv.at[z]).wait()

    def along(zz, i):
        return pltpu.make_async_remote_copy(
            src_ref=ra.at[z], dst_ref=ra.at[z], send_sem=z_send.at[i], recv_sem=a_recv.at[z],
            device_id=(dom(y, x, zz), e), device_id_type=MESH,
        )

    along(NZ - 1 - z // 2, 0).start()
    pl.when(z == 0)(along(1, 1).start)
    for i in (1, 2):
        zz = (z + i) % NZ
        pltpu.make_async_copy(ra.at[zz], ra.at[zz], a_recv.at[zz]).wait()

    for b in range(NY * NX * NZ // 2):
        pair = [ra[dd % NZ, dd // NZ].astype(f32) for dd in (2 * b, 2 * b + 1)]
        blk[b] = jnp.concatenate(halves(*pair), axis=0).astype(bf16)
    pltpu.make_async_copy(tl, tl, tl_sem).wait()
    small[2].wait()
    slot = x * NY + y
    for g in range(0, NY * NX, 8):
        group = peers[g:g + 8]
        for yy, xx in group:
            n = yy * NX + xx
            b = dom(yy, xx, z) // 2
            picked = jnp.concatenate([blk[cols_ref[t, b]] for t in range(NNZ)], axis=1)
            matrix = jnp.concatenate([tl[n, t] for t in range(NNZ)], axis=1)
            smooth = nt(picked, matrix)
            s3[n] = jnp.concatenate([smooth[:LG // 2], smooth[LG // 2:]], axis=1).astype(bf16)
        for peer in group:
            yy, xx = peer
            if peer is not peers[-1]:
                pltpu.make_async_remote_copy(
                    src_ref=s3.at[yy * NX + xx], dst_ref=r3.at[slot], send_sem=b_send, recv_sem=b_recv,
                    device_id=(dom(yy, xx, z), e), device_id_type=MESH,
                ).start()
            pltpu.make_async_remote_copy(
                src_ref=s3.at[yy * NX + xx], dst_ref=pr3.at[slot], send_sem=p_send, recv_sem=p_recv,
                device_id=(dom(yy, xx, z), zl * 2 + 1 - core), device_id_type=MESH,
            ).start()
    r3[slot] = s3[y * NX + x]
    arrived = r3.at[pl.ds(0, NY * NX - 1)]
    pltpu.make_async_copy(arrived, arrived, b_recv).wait()
    pltpu.make_async_copy(pr3, pr3, p_recv).wait()
    for j in range(NZL):
        pltpu.make_async_copy(pm.at[j], pm.at[j], pm_recv.at[j]).wait()

    def rows(field):
        tiles = [field[g * 8:(g + 1) * 8] for g in range(LEV // 8)]
        return jnp.concatenate(tiles[0::2] + tiles[1::2], axis=0)

    def packed(ref, s):
        return ref[s * NY:(s + 1) * NY].astype(f32).reshape(NY * LG // 2, 128).astype(bf16)

    local = jnp.concatenate([packed(ref, s) for ref in (r3, pr3) for s in range(4)], axis=0)
    none = jnp.zeros((NCO, OC), bf16)

    def term(s, field, back):
        at = slice(s * NY * LG // 2, (s + 1) * NY * LG // 2)
        return rows(field.astype(f32)) * jnp.concatenate([b[at] for b in back], axis=0)[:LEV]

    far = zl // 2
    targets = [3 * (1 - far), 2 - far, zl + 1 - 2 * (zl % 2), zl]
    kept = None
    for i, q in enumerate(targets):
        at = pl.ds(pl.multiple_of((q * 2 + core) * OC, OC), OC)
        hot = onehot[:, at]
        hot = jnp.concatenate([hot, none], axis=0), jnp.concatenate([none, hot], axis=0)
        back = [jnp.dot(local, h, preferred_element_type=f32) for h in hot]
        parts = [
            sum(term(k * 2 + c, mem[k * 2 + c, :, at], back) for k in range(2))
            + sum(term(4 + k * 2 + c, pm[q, k * 2 + c], back) for k in range(2))
            for c in range(2)
        ]
        both = jnp.concatenate(parts, axis=0)
        if i < NZL - 1:
            sc[i] = both.astype(bf16)
            pltpu.make_async_remote_copy(
                src_ref=sc.at[i], dst_ref=rb.at[zl], send_sem=c_send.at[i], recv_sem=c_recv.at[zl],
                device_id=(d, q * 2 + core), device_id_type=MESH,
            ).start()
        else:
            kept = both
    for i in (1, 3, 2):
        j = (zl + i) % NZL
        pltpu.make_async_copy(rb.at[j], rb.at[j], c_recv.at[j]).wait()
        kept = kept + rb[j].astype(f32)
    kept = kept / 15.0
    for c in range(2):
        tiles = [kept[c * LEV + g * 8:c * LEV + (g + 1) * 8] for g in range(LEV // 8)]
        first = (LEV // 8 + 1) // 2
        order = [tiles[g // 2 + first * (g % 2)] for g in range(LEV // 8)]
        out_ref[c] = jnp.concatenate(order, axis=0).astype(bf16)

    for ref, sem in ((r3, a_send), (r3, b_send)):
        sent = ref.at[pl.ds(0, NY * NX - 1)]
        pltpu.make_async_copy(sent, sent, sem).wait()
    pltpu.make_async_copy(ra.at[0], ra.at[0], z_send.at[0]).wait()

    @pl.when(z == 0)
    def _():
        pltpu.make_async_copy(ra.at[0], ra.at[0], z_send.at[1]).wait()

    @pl.when(z != 0)
    def _():
        pltpu.make_async_copy(ra.at[0], ra.at[0], d_send).wait()

    for q in range(NZL):
        pltpu.make_async_copy(pm.at[q], pm.at[q], pm_send.at[q]).wait()
    pltpu.make_async_copy(pr3, pr3, p_send).wait()
    for i in range(NZL - 1):
        pltpu.make_async_copy(sc.at[i], sc.at[i], c_send.at[i]).wait()


def shards(members, increment, vert_loc, tiles, tile_cols, coarse_of):
    dma = pltpu.SemaphoreType.DMA
    vmem = pl.BlockSpec(memory_space=pltpu.VMEM)
    hbm = pl.BlockSpec(memory_space=pl.ANY)
    return pl.pallas_call(
        kernel,
        name="covary",
        out_shape=jax.ShapeDtypeStruct((2, LEV, OC), bf16),
        in_specs=[hbm] * 6,
        out_specs=vmem,
        scratch_shapes=[
            pltpu.VMEM((LEV, LEV), f32),
            pltpu.SMEM((NNZ, NY * NX * NZ // 2), jnp.int32),
            pltpu.VMEM((1, COLS), jnp.int32),
            pltpu.VMEM((4, LEV, COLS), bf16),
            pltpu.VMEM((2, LEV, COLS), bf16),
            pltpu.VMEM((NY * NX, NNZ, NCO, TILE), bf16),
            pltpu.VMEM((NCO, COLS), bf16),
            pltpu.VMEM((NY * NX, LG // 2, 128), bf16),
            pltpu.VMEM((NZ, NY * NX, LG // 2, 128), bf16),
            pltpu.VMEM((NY * NX * NZ // 2, LG, 128), bf16),
            pltpu.VMEM((NY * NX, LG // 2, 128), bf16),
            pltpu.VMEM((NY * NX, LG // 2, 128), bf16),
            pltpu.VMEM((NY * NX, LG // 2, 128), bf16),
            pltpu.VMEM((NZL, 4, LEV, OC), bf16),
            pltpu.VMEM((NZL - 1, 2 * LEV, OC), bf16),
            pltpu.VMEM((NZL, 2 * LEV, OC), bf16),
            dma((3,)), dma((COLS // CH, 2)), dma,
            dma, dma, dma((NZ,)), dma((2,)), dma, dma,
            dma((NZL,)), dma((NZL,)), dma, dma, dma((NZL - 1,)), dma((NZL,)),
            pltpu.SemaphoreType.REGULAR,
        ],
        compiler_params=pltpu.CompilerParams(
            collective_id=0, has_side_effects=True, vmem_limit_bytes=63 * 2**20
        ),
    )(
        members.reshape(4, LEV, COLS), increment, vert_loc, tiles, tile_cols.T,
        coarse_of.reshape(1, COLS),
    )


def solution(mesh):
    return jax.shard_map(
        shards,
        mesh=mesh,
        in_specs=(P("ens", None, None, "dom"), P(None, None, "dom"), P(), P(), P(), P("dom")),
        out_specs=P(None, None, ("dom", "ens")),
        check_vma=False,
    )
```
